32 devices in a mesh: groups: 2 (over x), mp: 2 (over core), dp: 8 (over z, y).
Axes of the slice: x: 2, y: 2, z: 4, core: 2. Of those that a mesh axis runs over, the one named last changes fastest.
Arguments:
- activations: bfloat16 [4, 32, 4096], P(('groups', 'mp'), 'dp'), parts along dimension 0, may hold values from -6 to 6
- out_grads: bfloat16 [4, 32, 14336], P(('groups', 'mp'), 'dp'), parts along dimension 0, may hold values from -6 to 6
- slot_of: int32 [4, 32], P(('groups', 'mp'), 'dp'), parts along dimension 0, may hold values from 0 to 31, each once within a row
- lengths: int32 [4, 4], P(('groups', 'mp')), parts along dimension 0, may hold values from 1 to 10, 32 in all within a row
- weights: bfloat16 [4, 4096, 14336], P(('groups', 'mp'), 'dp'), parts along dimension 0, may hold values from -6 to 6
Outputs:
- merged: float32 [8192, 14336], P(('groups', 'dp'), 'mp'), parts along dimension 0
The draws below stay inside these ranges and needn't reach their ends.
There are 2 independent parts, one for each index of `groups`. The reference program is written for one: setup_inputs(seed, part) draws one part's arguments, and reference() takes and returns one part's arrays. A program takes and returns all parts, laid end to end along the dimension named above; each array names one. Nothing has to cross between parts.
Inputs may be any that keep to these rules, and one draw needn't show every extreme that they name: `slot_of`: each model's row is a permutation of 0..31. Each model's lengths sum to 32 and the largest is 10.
All inputs are finite; a program needn't handle non-finite values.
Results may differ from the reference program's by a relative error of at most 0.0003.
Values may be sent and summed in bfloat16 or wider, within the bound.
A program may use at most 256 MiB of HBM per device.

```python
import math
import jax
import jax.numpy as jnp
import numpy as np
from jax import lax

D = 4096
FF = 14336
EXAMPLES = 4
MODELS = 2
TOKENS = 32
LMAX = 10


def level_of(own_key, extent, split, smallest, largest):
    gain = 1.0
    for dim, shards_of in split:
        heights = jax.random.uniform(jax.random.fold_in(jax.random.fold_in(own_key, 6), dim), (shards_of,), jnp.float32, smallest / len(split), largest / len(split))
        gain = gain * jnp.repeat(jnp.exp(heights), extent[dim] // shards_of).reshape((-1,) + (1,) * (len(extent) - 1 - dim))
    return gain


def profile(count, total, most, lean):
    portions = [(1 << 20) // math.isqrt(rank ** lean) + 1 for rank in range(2, count + 1)]
    rest, counts = total - most - (count - 1), [1] * (count - 1)
    while rest > 0:
        movable = [i for i in range(count - 1) if counts[i] < most]
        mass, remaining = sum([portions[i] for i in movable]), rest
        for i in movable:
            more = min(most - counts[i], max(1, remaining * portions[i] // mass), rest)
            counts[i] = counts[i] + more
            rest = rest - more
    return np.array([most] + counts)


def uneven_parts(own_key, amount, total, bound, slope):
    if amount == 2:
        one = jax.random.randint(own_key, (), max(1, total - bound), min(bound, total - 1) + 1)
        return jnp.stack([one, total - one])
    tallies = jnp.asarray(profile(amount, total, bound, slope), jnp.int32)
    couples = (amount - 1) // 2
    donor, sink = tallies[1:1 + 2 * couples:2], tallies[2:2 + 2 * couples:2]
    slack = jnp.minimum(donor - 1, bound - sink)
    passed = jax.random.randint(jax.random.fold_in(own_key, 1), (couples,), 0, 1 << 20) % (slack + 1)
    tallies = tallies.at[1:1 + 2 * couples:2].set(donor - passed).at[2:2 + 2 * couples:2].set(sink + passed)
    return tallies[jax.random.permutation(jax.random.fold_in(own_key, 2), amount)]


def noise(key, extent, deviation, reach, split=(), held_as=jnp.bfloat16):
    drawn = jax.random.normal(key, extent, jnp.float32) * deviation
    if len(split) > 0:
        drawn = level_of(key, extent, split, -0.22, 0.18) * drawn
    return jnp.clip(drawn, min=-reach, max=reach).astype(held_as)


def setup_inputs(seed: int = 0, part: int = 0) -> dict:
    key_list = jax.random.split(jax.random.key(seed), 6)
    part_splits = jax.random.split(jax.random.fold_in(key_list[5], part), 6)
    return {
        "activations": noise(part_splits[0], (MODELS, TOKENS, D), 1.0, 6.0, ((0, 2), (1, 8))),
        "out_grads": noise(part_splits[1], (MODELS, TOKENS, FF), 1.0, 6.0, ((0, 2), (1, 8))),
        "slot_of": jax.vmap(lambda own: jax.random.permutation(own, TOKENS))(jax.random.split(part_splits[2], MODELS)).reshape((MODELS, TOKENS)).astype(jnp.int32),
        "lengths": jax.vmap(lambda own: uneven_parts(own, EXAMPLES, TOKENS, LMAX, 1))(jax.random.split(part_splits[3], MODELS)).reshape((MODELS, EXAMPLES)).astype(jnp.int32),
        "weights": noise(part_splits[4], (MODELS, D, FF), 1.0, 6.0, ((0, 2), (1, 8))),
    }


fisher_eps = 1e-8


def example_tables(lens, span):
    ends = jnp.cumsum(lens)
    starts = ends - lens
    offsets = jnp.arange(span, dtype=jnp.int32)
    live = offsets[None, :] < lens[:, None]
    source = jnp.where(live, starts[:, None] + offsets[None, :], 0).astype(jnp.int32)
    return source, live


def model_fisher(acts, grads, slots, lens):
    count = acts.shape[0]
    row_of = jnp.zeros((count,), jnp.int32).at[slots].set(jnp.arange(count, dtype=jnp.int32))
    source, live = example_tables(lens, LMAX)
    rows = row_of[source]

    def step(total, item):
        picks, keep = item
        left = jnp.where(keep[:, None], acts[picks], jnp.zeros((), jnp.bfloat16))
        right = grads[picks]
        grad = jnp.dot(left.T, right, preferred_element_type=jnp.float32)
        return total + grad * grad, None

    total, unused = lax.scan(step, jnp.zeros((acts.shape[1], grads.shape[1]), jnp.float32), (rows, live))
    return total


def reference(activations, out_grads, slot_of, lengths, weights):
    numerator = jnp.zeros((D, FF), jnp.float32)
    denominator = jnp.zeros((D, FF), jnp.float32)
    for model in range(MODELS):
        fisher = model_fisher(activations[model], out_grads[model], slot_of[model], lengths[model])
        numerator = numerator + fisher * weights[model].astype(jnp.float32)
        denominator = denominator + fisher
    return numerator / (denominator + fisher_eps)
```

```python
import functools

import jax
import jax.numpy as jnp
from jax import lax
from jax.experimental import pallas as pl
from jax.experimental.pallas import tpu as pltpu
from jax.sharding import PartitionSpec as P

EXAMPLES = 4
MODELS = 2
LANES = 128
DEPTH = 256
QUARTERS = 4
WIDE = 256
STACK = MODELS * EXAMPLES
SUB = 64

fisher_eps = 1e-08


def place_rows(all_slots, left_all, right_all):
    count = all_slots.shape[0]
    row_of = jnp.zeros((count,), jnp.int32).at[all_slots].set(jnp.arange(count, dtype=jnp.int32))
    return (left_all[row_of], right_all[row_of])


def fisher_block(left_ord, right_ord, lens, span):
    count = left_ord.shape[0]
    ends = jnp.cumsum(lens)
    starts = ends - lens
    offsets = jnp.arange(span, dtype=jnp.int32)
    total = jnp.zeros((left_ord.shape[1], right_ord.shape[1]), jnp.float32)
    for example in range(EXAMPLES):
        begin = starts[example]
        clamped = jnp.minimum(begin, count - span)
        where_at = clamped + offsets
        keep = (where_at >= begin) & (where_at < begin + lens[example])
        left = lax.dynamic_slice_in_dim(left_ord, clamped, span, 0)
        left = jnp.where(keep[:, None], left, jnp.zeros((), jnp.bfloat16))
        right = lax.dynamic_slice_in_dim(right_ord, clamped, span, 0)
        grad = jnp.dot(left.T, right, preferred_element_type=jnp.float32)
        total = total + grad * grad
    return total


def shards_general(activations, out_grads, slot_of, lengths, weights):
    acts = activations[0]
    grads = out_grads[0]
    slots = slot_of[0]
    lens = lengths[0]
    w_shard = weights[0]
    span = lax.axis_size("dp") * acts.shape[0] // 3
    x_block = lax.all_to_all(acts, "dp", split_axis=1, concat_axis=0, tiled=True)
    all_grads, all_slots = (
        lax.all_gather(grads, "dp", axis=0, tiled=True),
        lax.all_gather(slots, "dp", axis=0, tiled=True),
    )
    left_ord, right_ord = place_rows(all_slots, x_block, all_grads)
    fisher = fisher_block(left_ord, right_ord, lens, span)
    weighted = fisher * w_shard.astype(jnp.float32)
    num_half, den_half = (
        lax.psum_scatter(weighted, "mp", scatter_dimension=1, tiled=True),
        lax.psum_scatter(fisher, "mp", scatter_dimension=1, tiled=True),
    )
    return num_half / (den_half + fisher_eps)


def merge_kernel(sources, groups, x_ref, g_ref, w_ref, out_ref, x_all, g_all, lhs, w_own, w_mate, out_buf,
                 x_recv, g_recv, w_recv, own_sem, x_send, g_send, w_send, out_sem):
    mp, dp = lax.axis_index("mp"), lax.axis_index("dp")
    mate = 1 - mp
    mine = mp * sources + dp
    rows, cols = out_ref.shape
    chunks = g_ref.shape[1]
    step = QUARTERS * WIDE

    def w_copy(c):
        return pltpu.make_async_remote_copy(
            src_ref=w_ref.at[:, pl.ds(pl.multiple_of(mate * cols + c * step, LANES), step)],
            dst_ref=w_mate.at[:, pl.ds(c * step, step)],
            send_sem=w_send.at[c],
            recv_sem=w_recv.at[c],
            device_id={"mp": mate},
            device_id_type=pl.DeviceIdType.MESH,
        )

    def own_copy(c):
        return pltpu.make_async_copy(
            w_ref.at[:, pl.ds(pl.multiple_of(mp * cols + c * step, LANES), step)],
            w_own.at[:, pl.ds(c * step, step)],
            own_sem.at[c],
        )

    def out_copy(c):
        return pltpu.make_async_copy(
            out_buf.at[c % 2], out_ref.at[:, pl.ds(c * step, step)], out_sem.at[c % 2])

    partners = [(i, k) for k in range(sources) for i in range(MODELS) if (i, k) != (0, 0)]
    places = [(lax.rem(mp + i, MODELS), lax.rem(dp + k, sources)) for i, k in partners]

    barrier = pltpu.get_barrier_semaphore()
    for to_mp, to_dp in places:
        pl.semaphore_signal(barrier, inc=1, device_id={"mp": to_mp, "dp": to_dp},
                            device_id_type=pl.DeviceIdType.MESH)
    pltpu.make_async_copy(x_ref.at[dp], x_all.at[mine], x_recv).start()
    for n, (lo, hi) in enumerate(groups):
        pltpu.make_async_copy(g_ref.at[mp, pl.ds(lo, hi - lo)], g_all.at[pl.ds(lo, hi - lo), mine],
                              g_recv.at[n]).start()
    for c in range(chunks):
        own_copy(c).start()
    pl.semaphore_wait(barrier, len(places))

    for to_mp, to_dp in places:
        pltpu.make_async_remote_copy(
            src_ref=x_ref.at[to_dp], dst_ref=x_all.at[mine], send_sem=x_send, recv_sem=x_recv,
            device_id={"mp": to_mp, "dp": to_dp}, device_id_type=pl.DeviceIdType.MESH).start()
    w_copy(0).start()
    for n, (lo, hi) in enumerate(groups):
        for to_mp, to_dp in places:
            pltpu.make_async_remote_copy(
                src_ref=g_ref.at[to_mp, pl.ds(lo, hi - lo)], dst_ref=g_all.at[pl.ds(lo, hi - lo), mine],
                send_sem=g_send.at[n], recv_sem=g_recv.at[n],
                device_id={"mp": to_mp, "dp": to_dp}, device_id_type=pl.DeviceIdType.MESH).start()
        if n == 0:
            for c in range(1, chunks):
                w_copy(c).start()

    pltpu.make_async_copy(x_all, x_all, x_recv).wait()
    turned = x_all[...].reshape(DEPTH, -1).astype(jnp.float32).T
    code = turned[rows:rows + 1, :]
    left = turned[:rows, :].astype(jnp.bfloat16)
    for q in range(QUARTERS):
        for v in range(STACK):
            which = lax.rem(mp + v // EXAMPLES, MODELS) * EXAMPLES + v % EXAMPLES
            keep = code == (which * QUARTERS + q).astype(jnp.float32)
            part = left * keep.astype(jnp.float32).astype(jnp.bfloat16)
            for t in range(rows // SUB):
                lhs[q, t, v * SUB:(v + 1) * SUB, :] = part[t * SUB:(t + 1) * SUB, :]

    starts = {lo: n for n, (lo, hi) in enumerate(groups)}
    for c in range(chunks):
        if c in starts:
            lo, hi = groups[starts[c]]
            whole = g_all.at[pl.ds(lo, hi - lo)]
            pltpu.make_async_copy(whole, whole, g_recv.at[starts[c]]).wait()
        own_copy(c).wait()
        w_copy(c).wait_recv()
        if c >= 2:
            out_copy(c - 2).wait()

        @pl.loop(0, rows // SUB)
        def _(t):
            at = pl.multiple_of(t * SUB, SUB)
            for q in range(QUARTERS):
                right = g_all[c].reshape(DEPTH, WIDE)
                grads = jnp.dot(lhs[q, t], right, preferred_element_type=jnp.float32)
                square = grads * grads
                own, other = [
                    sum(square[(h * EXAMPLES + e) * SUB:(h * EXAMPLES + e + 1) * SUB] for e in range(EXAMPLES))
                    for h in range(MODELS)
                ]
                here = pl.ds(c * step + q * WIDE, WIDE)
                top = (own * w_own[pl.ds(at, SUB), here].astype(jnp.float32)
                       + other * w_mate[pl.ds(at, SUB), here].astype(jnp.float32))
                out_buf[c % 2, pl.ds(at, SUB), q * WIDE:(q + 1) * WIDE] = top / (own + other + fisher_eps)

        out_copy(c).start()

    for c in range(max(0, chunks - 2), chunks):
        out_copy(c).wait()
    for c in range(chunks):
        w_copy(c).wait_send()
    sent = x_all.at[pl.ds(0, len(places))]
    pltpu.make_async_copy(sent, sent, x_send).wait()
    for n, (lo, hi) in enumerate(groups):
        sent = g_all.at[pl.ds(lo, hi - lo), pl.ds(0, len(places))]
        pltpu.make_async_copy(sent, sent, g_send.at[n]).wait()


def shards_kernel(activations, out_grads, slot_of, lengths, weights):
    acts, grads, slots, lens, w_shard = activations[0], out_grads[0], slot_of[0], lengths[0], weights[0]
    sources = lax.axis_size("dp")
    tokens, width = acts.shape
    rows = width // sources
    cols = grads.shape[1] // MODELS
    chunks = cols // (QUARTERS * WIDE)
    packed = QUARTERS * tokens
    example = jnp.sum((slots[:, None] >= jnp.cumsum(lens)[None, :]).astype(jnp.int32), axis=1)
    code = (lax.axis_index("mp") * EXAMPLES + example)[None, :] * QUARTERS + jnp.arange(QUARTERS)[:, None]
    x_part = acts.reshape(tokens, sources, rows).transpose(1, 0, 2)
    x_part = jnp.broadcast_to(x_part[:, None], (sources, QUARTERS, tokens, rows)).reshape(sources, packed, rows)
    code = jnp.broadcast_to(code.reshape(1, packed, 1), (sources, packed, LANES)).astype(jnp.bfloat16)
    x_pack = jnp.concatenate([x_part, code], axis=2)
    g_pack = grads.reshape(tokens, MODELS, chunks, QUARTERS, WIDE).transpose(1, 2, 3, 0, 4)
    g_pack = g_pack.reshape(MODELS, chunks, packed, WIDE)
    groups = ((0, 1), (1, 3), (3, chunks))
    everyone = MODELS * sources
    step = QUARTERS * WIDE
    dma = pltpu.SemaphoreType.DMA
    return pl.pallas_call(
        functools.partial(merge_kernel, sources, groups),
        out_shape=jax.ShapeDtypeStruct((rows, cols), jnp.float32),
        in_specs=[pl.BlockSpec(memory_space=pl.ANY)] * 3,
        out_specs=pl.BlockSpec(memory_space=pl.ANY),
        scratch_shapes=[
            pltpu.VMEM((everyone, packed, rows + LANES), jnp.bfloat16),
            pltpu.VMEM((chunks, everyone, packed, WIDE), jnp.bfloat16),
            pltpu.VMEM((QUARTERS, rows // SUB, STACK * SUB, DEPTH), jnp.bfloat16),
            pltpu.VMEM((rows, cols), jnp.bfloat16),
            pltpu.VMEM((rows, cols), jnp.bfloat16),
            pltpu.VMEM((2, rows, step), jnp.float32),
            dma, dma((len(groups),)), dma((chunks,)), dma((chunks,)),
            dma, dma((len(groups),)), dma((chunks,)), dma((2,)),
        ],
        compiler_params=pltpu.CompilerParams(
            collective_id=0, has_side_effects=True, vmem_limit_bytes=56 * 1024 * 1024),
        cost_estimate=pl.CostEstimate(
            flops=2 * STACK * rows * cols * DEPTH, bytes_accessed=12 * rows * cols, transcendentals=0),
        name="merge",
    )(x_pack, g_pack, w_shard)


def solution(mesh):
    in_specs = (
        P(("groups", "mp"), "dp", None),
        P(("groups", "mp"), "dp", None),
        P(("groups", "mp"), "dp"),
        P(("groups", "mp"), None),
        P(("groups", "mp"), "dp", None),
    )
    out_specs = P(("groups", "dp"), "mp")

    def merge(activations, out_grads, slot_of, lengths, weights):
        tokens = activations.shape[1]
        rows = activations.shape[2] // mesh.shape["dp"]
        cols = out_grads.shape[2] // MODELS
        fits = (MODELS * QUARTERS * tokens == DEPTH and (QUARTERS * tokens // mesh.shape["dp"]) % 16 == 0
                and rows % SUB == 0 and cols % (QUARTERS * WIDE) == 0 and cols // (QUARTERS * WIDE) > 3)
        body = shards_kernel if fits else shards_general
        return jax.shard_map(body, mesh=mesh, in_specs=in_specs, out_specs=out_specs, check_vma=False)(
            activations, out_grads, slot_of, lengths, weights)

    return merge
```

```python
import functools

import jax
import jax.numpy as jnp
from jax import lax
from jax.experimental import pallas as pl
from jax.experimental.pallas import tpu as pltpu
from jax.sharding import PartitionSpec as P

EXAMPLES = 4
MODELS = 2
LANES = 128
DEPTH = 256
QUARTERS = 4
WIDE = 256
STACK = MODELS * EXAMPLES
SUB = 256
LINES = 2

fisher_eps = 1e-08


def place_rows(all_slots, left_all, right_all):
    count = all_slots.shape[0]
    row_of = jnp.zeros((count,), jnp.int32).at[all_slots].set(jnp.arange(count, dtype=jnp.int32))
    return (left_all[row_of], right_all[row_of])


def fisher_block(left_ord, right_ord, lens, span):
    count = left_ord.shape[0]
    ends = jnp.cumsum(lens)
    starts = ends - lens
    offsets = jnp.arange(span, dtype=jnp.int32)
    total = jnp.zeros((left_ord.shape[1], right_ord.shape[1]), jnp.float32)
    for example in range(EXAMPLES):
        begin = starts[example]
        clamped = jnp.minimum(begin, count - span)
        where_at = clamped + offsets
        keep = (where_at >= begin) & (where_at < begin + lens[example])
        left = lax.dynamic_slice_in_dim(left_ord, clamped, span, 0)
        left = jnp.where(keep[:, None], left, jnp.zeros((), jnp.bfloat16))
        right = lax.dynamic_slice_in_dim(right_ord, clamped, span, 0)
        grad = jnp.dot(left.T, right, preferred_element_type=jnp.float32)
        total = total + grad * grad
    return total


def shards_general(activations, out_grads, slot_of, lengths, weights):
    acts = activations[0]
    grads = out_grads[0]
    slots = slot_of[0]
    lens = lengths[0]
    w_shard = weights[0]
    span = lax.axis_size("dp") * acts.shape[0] // 3
    x_block = lax.all_to_all(acts, "dp", split_axis=1, concat_axis=0, tiled=True)
    all_grads, all_slots = (
        lax.all_gather(grads, "dp", axis=0, tiled=True),
        lax.all_gather(slots, "dp", axis=0, tiled=True),
    )
    left_ord, right_ord = place_rows(all_slots, x_block, all_grads)
    fisher = fisher_block(left_ord, right_ord, lens, span)
    weighted = fisher * w_shard.astype(jnp.float32)
    num_half, den_half = (
        lax.psum_scatter(weighted, "mp", scatter_dimension=1, tiled=True),
        lax.psum_scatter(fisher, "mp", scatter_dimension=1, tiled=True),
    )
    return num_half / (den_half + fisher_eps)


def merge_kernel(sources, x_ref, g_ref, w_ref, out_ref, x_all, g_all, lhs, w_own, w_mate,
                 x_recv, line_recv, relay_recv, w_recv, own_sem, x_send, line_send, relay_send, w_send):
    mp, dp = lax.axis_index("mp"), lax.axis_index("dp")
    mate = 1 - mp
    line, spot = lax.rem(dp, LINES), lax.div(dp, LINES)
    length = sources // LINES
    rows, cols = out_ref.shape
    chunks = g_ref.shape[1]
    step = QUARTERS * WIDE

    def send(src, dst, send_sem, recv_sem, to_mp, to_dp):
        return pltpu.make_async_remote_copy(
            src_ref=src, dst_ref=dst, send_sem=send_sem, recv_sem=recv_sem,
            device_id={"mp": to_mp, "dp": to_dp}, device_id_type=pl.DeviceIdType.MESH)

    def w_copy(c):
        return send(w_ref.at[:, pl.ds(pl.multiple_of(mate * cols + c * step, LANES), step)],
                    w_mate.at[:, pl.ds(pl.multiple_of(c * step, LANES), step)],
                    w_send.at[c], w_recv.at[c], mate, dp)

    def own_copy(c):
        return pltpu.make_async_copy(
            w_ref.at[:, pl.ds(pl.multiple_of(mp * cols + c * step, LANES), step)],
            w_own.at[:, pl.ds(pl.multiple_of(c * step, LANES), step)],
            own_sem.at[c])

    def line_copy(c, to_mp, to_dp):
        return send(g_ref.at[to_mp, c], g_all.at[c, line, spot, mp], line_send.at[c], line_recv.at[c], to_mp, to_dp)

    def relay_copy(c):
        return send(g_all.at[c, line], g_all.at[c, line], relay_send.at[c], relay_recv.at[c],
                    mp, spot * LINES + 1 - line)

    def relay(c):
        whole = g_all.at[c, line]
        pltpu.make_async_copy(whole, whole, line_recv.at[c]).wait()
        relay_copy(c).start()

    offsets = [(i, k) for k in range(sources) for i in range(MODELS) if (i, k) != (0, 0)]
    places = [(lax.rem(mp + i, MODELS), lax.rem(dp + k, sources)) for i, k in offsets]
    in_line = [(lax.rem(mp + i, MODELS), lax.rem(dp + k * LINES, sources))
               for k in range(length) for i in range(MODELS) if (i, k) != (0, 0)]

    barrier = pltpu.get_barrier_semaphore()
    for to_mp, to_dp in places:
        pl.semaphore_signal(barrier, inc=1, device_id={"mp": to_mp, "dp": to_dp},
                            device_id_type=pl.DeviceIdType.MESH)
    pltpu.make_async_copy(x_ref.at[dp], x_all.at[line, spot, mp], x_recv).start()

    @pl.loop(0, chunks)
    def _(c):
        pltpu.make_async_copy(g_ref.at[mp, c], g_all.at[c, line, spot, mp], line_recv.at[c]).start()
        own_copy(c).start()

    pl.semaphore_wait(barrier, len(places))
    for to_mp, to_dp in in_line:
        line_copy(0, to_mp, to_dp).start()
    for to_mp, to_dp in places:
        send(x_ref.at[to_dp], x_all.at[line, spot, mp], x_send, x_recv, to_mp, to_dp).start()
    w_copy(0).start()

    @pl.loop(1, chunks)
    def _(c):
        for to_mp, to_dp in in_line:
            line_copy(c, to_mp, to_dp).start()
        w_copy(c).start()

    relay(0)
    relay(1)

    pltpu.make_async_copy(x_all, x_all, x_recv).wait()
    arrived = x_all[...].reshape(DEPTH, 2 * LANES).astype(jnp.float32).T
    code = arrived[LANES:LANES + 1, :]
    arrived = arrived[:LANES, :].astype(jnp.bfloat16)
    tokens = DEPTH // (MODELS * sources * QUARTERS)
    packed = QUARTERS * tokens
    source = lax.broadcasted_iota(jnp.int32, (DEPTH, DEPTH), 0)
    target = lax.broadcasted_iota(jnp.int32, (DEPTH, DEPTH), 1)
    same = (source // packed == target // packed) & (source % tokens == target % tokens)
    for p in range(rows // LANES):
        spread = (same & (source % packed // tokens == p)).astype(jnp.float32).astype(jnp.bfloat16)
        left = jnp.dot(arrived, spread, preferred_element_type=jnp.float32).astype(jnp.bfloat16)
        t, base = p * LANES // SUB, p * LANES % SUB
        for q in range(QUARTERS):
            for v in range(STACK):
                which = lax.rem(mp + v // EXAMPLES, MODELS) * EXAMPLES + v % EXAMPLES
                keep = code == (which * QUARTERS + q).astype(jnp.float32)
                lhs[q, t, v * SUB + base:v * SUB + base + LANES, :] = left * keep.astype(jnp.float32).astype(jnp.bfloat16)

    @pl.loop(0, chunks)
    def _(c):
        @pl.when(c + 2 < chunks)
        def _():
            relay(c + 2)

        other_line = g_all.at[c, 1 - line]
        pltpu.make_async_copy(other_line, other_line, relay_recv.at[c]).wait()
        own_copy(c).wait()
        w_copy(c).wait_recv()

        @pl.loop(0, rows // SUB)
        def _(t):
            at = pl.ds(pl.multiple_of(t * SUB, SUB), SUB)
            for q in range(QUARTERS):
                right = g_all[c].reshape(DEPTH, WIDE)
                fishers = []
                for h in range(MODELS):
                    fisher = jnp.zeros((SUB, WIDE), jnp.float32)
                    for e in range(EXAMPLES):
                        v = h * EXAMPLES + e
                        grad = jnp.dot(lhs[q, t, v * SUB:(v + 1) * SUB, :], right, preferred_element_type=jnp.float32)
                        fisher = fisher + grad * grad
                    fishers.append(fisher)
                own, other = fishers
                here = pl.ds(pl.multiple_of(c * step + q * WIDE, LANES), WIDE)
                top = own * w_own[at, here].astype(jnp.float32) + other * w_mate[at, here].astype(jnp.float32)
                out_ref[at, here] = top / (own + other + fisher_eps)

    blocks = lambda count: lhs.at[0, 0, pl.ds(0, count * packed)]
    pltpu.make_async_copy(blocks(len(places)), blocks(len(places)), x_send).wait()

    @pl.loop(0, chunks)
    def _(c):
        pltpu.make_async_copy(blocks(len(in_line)), blocks(len(in_line)), line_send.at[c]).wait()
        relay_copy(c).wait_send()
        w_copy(c).wait_send()


def shards_kernel(activations, out_grads, slot_of, lengths, weights):
    acts, grads, slots, lens, w_shard = activations[0], out_grads[0], slot_of[0], lengths[0], weights[0]
    sources = lax.axis_size("dp")
    tokens, width = acts.shape
    rows = width // sources
    cols = grads.shape[1] // MODELS
    chunks = cols // (QUARTERS * WIDE)
    packed = QUARTERS * tokens
    example, end = jnp.zeros((tokens,), jnp.int32), 0
    for e in range(EXAMPLES - 1):
        end = end + lens[e]
        example = example + (slots >= end).astype(jnp.int32)
    code = (lax.axis_index("mp") * EXAMPLES + example)[None, :] * QUARTERS + jnp.arange(QUARTERS)[:, None]
    x_part = acts.reshape(tokens, sources, rows // LANES, LANES).transpose(1, 2, 0, 3).reshape(sources, packed, LANES)
    code = jnp.broadcast_to(code.reshape(1, packed, 1), (sources, packed, LANES)).astype(jnp.bfloat16)
    x_pack = jnp.concatenate([x_part, code], axis=2)
    g_pack = grads.reshape(tokens, MODELS, chunks, QUARTERS, WIDE).transpose(1, 2, 3, 0, 4)
    g_pack = g_pack.reshape(MODELS, chunks, packed, WIDE)
    length = sources // LINES
    dma = pltpu.SemaphoreType.DMA
    return pl.pallas_call(
        functools.partial(merge_kernel, sources),
        out_shape=pltpu.VMEM((rows, cols), jnp.float32),
        in_specs=[pl.BlockSpec(memory_space=pl.ANY)] * 3,
        out_specs=pl.BlockSpec(memory_space=pltpu.VMEM),
        scratch_shapes=[
            pltpu.VMEM((LINES, length, MODELS, packed, 2 * LANES), jnp.bfloat16),
            pltpu.VMEM((chunks, LINES, length, MODELS, packed, WIDE), jnp.bfloat16),
            pltpu.VMEM((QUARTERS, rows // SUB, STACK * SUB, DEPTH), jnp.bfloat16),
            pltpu.VMEM((rows, cols), jnp.bfloat16),
            pltpu.VMEM((rows, cols), jnp.bfloat16),
            dma, dma((chunks,)), dma((chunks,)), dma((chunks,)), dma((chunks,)),
            dma, dma((chunks,)), dma((chunks,)), dma((chunks,)),
        ],
        compiler_params=pltpu.CompilerParams(
            collective_id=0, has_side_effects=True, vmem_limit_bytes=40 * 1024 * 1024),
        cost_estimate=pl.CostEstimate(
            flops=2 * STACK * rows * cols * DEPTH, bytes_accessed=12 * rows * cols, transcendentals=0),
        name="merge",
    )(x_pack, g_pack, w_shard)


def solution(mesh):
    in_specs = (
        P(("groups", "mp"), "dp", None),
        P(("groups", "mp"), "dp", None),
        P(("groups", "mp"), "dp"),
        P(("groups", "mp"), None),
        P(("groups", "mp"), "dp", None),
    )
    out_specs = P(("groups", "dp"), "mp")

    def merge(activations, out_grads, slot_of, lengths, weights):
        tokens = activations.shape[1]
        rows = activations.shape[2] // mesh.shape["dp"]
        cols = out_grads.shape[2] // MODELS
        fits = (MODELS * QUARTERS * tokens == DEPTH and (QUARTERS * tokens // mesh.shape["dp"]) % 16 == 0
                and rows % SUB == 0 and rows == QUARTERS * LANES and cols % (QUARTERS * WIDE) == 0 and cols // (QUARTERS * WIDE) > 3)
        body = shards_kernel if fits else shards_general
        return jax.shard_map(body, mesh=mesh, in_specs=in_specs, out_specs=out_specs, check_vma=False)(
            activations, out_grads, slot_of, lengths, weights)

    return merge
```

```python
import functools

import jax
import jax.numpy as jnp
from jax import lax
from jax.experimental import pallas as pl
from jax.experimental.pallas import tpu as pltpu
from jax.sharding import PartitionSpec as P

EXAMPLES = 4
MODELS = 2
LANES = 128
DEPTH = 256
QUARTERS = 4
WIDE = 256
STACK = MODELS * EXAMPLES
SUB = 256
LINES = 2

fisher_eps = 1e-08


def place_rows(all_slots, left_all, right_all):
    count = all_slots.shape[0]
    row_of = jnp.zeros((count,), jnp.int32).at[all_slots].set(jnp.arange(count, dtype=jnp.int32))
    return (left_all[row_of], right_all[row_of])


def fisher_block(left_ord, right_ord, lens, span):
    count = left_ord.shape[0]
    ends = jnp.cumsum(lens)
    starts = ends - lens
    offsets = jnp.arange(span, dtype=jnp.int32)
    total = jnp.zeros((left_ord.shape[1], right_ord.shape[1]), jnp.float32)
    for example in range(EXAMPLES):
        begin = starts[example]
        clamped = jnp.minimum(begin, count - span)
        where_at = clamped + offsets
        keep = (where_at >= begin) & (where_at < begin + lens[example])
        left = lax.dynamic_slice_in_dim(left_ord, clamped, span, 0)
        left = jnp.where(keep[:, None], left, jnp.zeros((), jnp.bfloat16))
        right = lax.dynamic_slice_in_dim(right_ord, clamped, span, 0)
        grad = jnp.dot(left.T, right, preferred_element_type=jnp.float32)
        total = total + grad * grad
    return total


def shards_general(activations, out_grads, slot_of, lengths, weights):
    acts = activations[0]
    grads = out_grads[0]
    slots = slot_of[0]
    lens = lengths[0]
    w_shard = weights[0]
    span = lax.axis_size("dp") * acts.shape[0] // 3
    x_block = lax.all_to_all(acts, "dp", split_axis=1, concat_axis=0, tiled=True)
    all_grads, all_slots = (
        lax.all_gather(grads, "dp", axis=0, tiled=True),
        lax.all_gather(slots, "dp", axis=0, tiled=True),
    )
    left_ord, right_ord = place_rows(all_slots, x_block, all_grads)
    fisher = fisher_block(left_ord, right_ord, lens, span)
    weighted = fisher * w_shard.astype(jnp.float32)
    num_half, den_half = (
        lax.psum_scatter(weighted, "mp", scatter_dimension=1, tiled=True),
        lax.psum_scatter(fisher, "mp", scatter_dimension=1, tiled=True),
    )
    return num_half / (den_half + fisher_eps)


def merge_kernel(sources, slots_ref, lens_ref, acts_ref, grads_ref, w_ref, out_ref, x_ref, g_ref, x_all, g_all, lhs, w_own, w_mate,
                 x_recv, line_recv, relay_recv, w_recv, own_sem, x_send, line_send, relay_send, w_send):
    mp, dp = lax.axis_index("mp"), lax.axis_index("dp")
    mate = 1 - mp
    line, spot = lax.rem(dp, LINES), lax.div(dp, LINES)
    length = sources // LINES
    rows, cols = out_ref.shape
    chunks = g_ref.shape[1]
    step = QUARTERS * WIDE

    def send(src, dst, send_sem, recv_sem, to_mp, to_dp):
        return pltpu.make_async_remote_copy(
            src_ref=src, dst_ref=dst, send_sem=send_sem, recv_sem=recv_sem,
            device_id={"mp": to_mp, "dp": to_dp}, device_id_type=pl.DeviceIdType.MESH)

    def w_copy(c):
        return send(w_ref.at[:, pl.ds(pl.multiple_of(mate * cols + c * step, LANES), step)],
                    w_mate.at[:, pl.ds(pl.multiple_of(c * step, LANES), step)],
                    w_send.at[c], w_recv.at[c], mate, dp)

    def own_copy(c):
        return pltpu.make_async_copy(
            w_ref.at[:, pl.ds(pl.multiple_of(mp * cols + c * step, LANES), step)],
            w_own.at[:, pl.ds(pl.multiple_of(c * step, LANES), step)],
            own_sem.at[c])

    def line_copy(c, to_mp, to_dp):
        return send(g_ref.at[to_mp, c], g_all.at[c, line, spot, mp], line_send.at[c], line_recv.at[c], to_mp, to_dp)

    def relay_copy(c):
        return send(g_all.at[c, line], g_all.at[c, line], relay_send.at[c], relay_recv.at[c],
                    mp, spot * LINES + 1 - line)

    def relay(c):
        whole = g_all.at[c, line]
        pltpu.make_async_copy(whole, whole, line_recv.at[c]).wait()
        relay_copy(c).start()

    offsets = [(i, k) for k in range(sources) for i in range(MODELS) if (i, k) != (0, 0)]
    places = [(lax.rem(mp + i, MODELS), lax.rem(dp + k, sources)) for i, k in offsets]
    in_line = [(lax.rem(mp + i, MODELS), lax.rem(dp + k * LINES, sources))
               for k in range(length) for i in range(MODELS) if (i, k) != (0, 0)]

    barrier = pltpu.get_barrier_semaphore()
    for to_mp, to_dp in places:
        pl.semaphore_signal(barrier, inc=1, device_id={"mp": to_mp, "dp": to_dp},
                            device_id_type=pl.DeviceIdType.MESH)

    tokens = acts_ref.shape[0]
    packed = QUARTERS * tokens
    row = lax.broadcasted_iota(jnp.int32, (packed, LANES), 0)
    code = row // tokens
    for i in range(tokens):
        end, example = 0, 0
        for e in range(EXAMPLES - 1):
            end = end + lens_ref[0, e]
            example = example + jnp.where(slots_ref[0, i] >= end, 1, 0)
        code = code + jnp.where(row % tokens == i, (mp * EXAMPLES + example) * QUARTERS, 0)
    code = code.astype(jnp.float32).astype(jnp.bfloat16)

    def stacked(ref, start, width):
        parts = [ref[:, start + q * width:start + (q + 1) * width].astype(jnp.float32) for q in range(QUARTERS)]
        return jnp.concatenate(parts, axis=0).astype(jnp.bfloat16)

    for m in range(MODELS):
        for c in range(chunks):
            g_ref[m, c] = stacked(grads_ref, m * cols + c * step, WIDE)
    for k in range(sources):
        x_ref[k, :, :LANES] = stacked(acts_ref, k * rows, LANES)
        x_ref[k, :, LANES:] = code

    pltpu.make_async_copy(x_ref.at[dp], x_all.at[line, spot, mp], x_recv).start()

    @pl.loop(0, chunks)
    def _(c):
        pltpu.make_async_copy(g_ref.at[mp, c], g_all.at[c, line, spot, mp], line_recv.at[c]).start()
        own_copy(c).start()

    pl.semaphore_wait(barrier, len(places))
    for to_mp, to_dp in in_line:
        line_copy(0, to_mp, to_dp).start()
    for to_mp, to_dp in places:
        send(x_ref.at[to_dp], x_all.at[line, spot, mp], x_send, x_recv, to_mp, to_dp).start()
    w_copy(0).start()

    @pl.loop(1, chunks)
    def _(c):
        for to_mp, to_dp in in_line:
            line_copy(c, to_mp, to_dp).start()
        w_copy(c).start()

    relay(0)
    relay(1)

    pltpu.make_async_copy(x_all, x_all, x_recv).wait()
    arrived = x_all[...].reshape(DEPTH, 2 * LANES).astype(jnp.float32).T
    marks = arrived[LANES:LANES + 1, :]
    arrived = arrived[:LANES, :].astype(jnp.bfloat16)
    source = lax.broadcasted_iota(jnp.int32, (DEPTH, DEPTH), 0)
    target = lax.broadcasted_iota(jnp.int32, (DEPTH, DEPTH), 1)
    same = (source // packed == target // packed) & (source % tokens == target % tokens)
    for p in range(rows // LANES):
        spread = (same & (source % packed // tokens == p)).astype(jnp.float32).astype(jnp.bfloat16)
        left = jnp.dot(arrived, spread, preferred_element_type=jnp.float32).astype(jnp.bfloat16)
        t, base = p * LANES // SUB, p * LANES % SUB
        for q in range(QUARTERS):
            for v in range(STACK):
                which = lax.rem(mp + v // EXAMPLES, MODELS) * EXAMPLES + v % EXAMPLES
                keep = marks == (which * QUARTERS + q).astype(jnp.float32)
                lhs[q, t, v * SUB + base:v * SUB + base + LANES, :] = left * keep.astype(jnp.float32).astype(jnp.bfloat16)

    @pl.loop(0, chunks)
    def _(c):
        other_line = g_all.at[c, 1 - line]
        pltpu.make_async_copy(other_line, other_line, relay_recv.at[c]).wait()
        own_copy(c).wait()
        w_copy(c).wait_recv()

        @pl.loop(0, rows // SUB)
        def _(t):
            @pl.when((t == rows // SUB - 1) & (c + 2 < chunks))
            def _():
                relay(c + 2)

            at = pl.ds(pl.multiple_of(t * SUB, SUB), SUB)
            for q in range(QUARTERS):
                right = g_all[c].reshape(DEPTH, WIDE)
                fishers = []
                for h in range(MODELS):
                    fisher = jnp.zeros((SUB, WIDE), jnp.float32)
                    for e in range(EXAMPLES):
                        v = h * EXAMPLES + e
                        grad = jnp.dot(lhs[q, t, v * SUB:(v + 1) * SUB, :], right, preferred_element_type=jnp.float32)
                        fisher = fisher + grad * grad
                    fishers.append(fisher)
                own, other = fishers
                here = pl.ds(pl.multiple_of(c * step + q * WIDE, LANES), WIDE)
                top = own * w_own[at, here].astype(jnp.float32) + other * w_mate[at, here].astype(jnp.float32)
                out_ref[at, here] = top / (own + other + fisher_eps)

    blocks = lambda count: lhs.at[0, 0, pl.ds(0, count * packed)]
    pltpu.make_async_copy(blocks(len(places)), blocks(len(places)), x_send).wait()

    @pl.loop(0, chunks)
    def _(c):
        pltpu.make_async_copy(blocks(len(in_line)), blocks(len(in_line)), line_send.at[c]).wait()
        relay_copy(c).wait_send()
        w_copy(c).wait_send()


def shards_kernel(activations, out_grads, slot_of, lengths, weights):
    acts, grads, w_shard = activations[0], out_grads[0], weights[0]
    sources = lax.axis_size("dp")
    tokens, width = acts.shape
    rows = width // sources
    cols = grads.shape[1] // MODELS
    chunks = cols // (QUARTERS * WIDE)
    packed = QUARTERS * tokens
    length = sources // LINES
    dma = pltpu.SemaphoreType.DMA
    return pl.pallas_call(
        functools.partial(merge_kernel, sources),
        out_shape=pltpu.VMEM((rows, cols), jnp.float32),
        in_specs=[
            pl.BlockSpec(memory_space=pltpu.SMEM), pl.BlockSpec(memory_space=pltpu.SMEM),
            pl.BlockSpec(memory_space=pltpu.VMEM), pl.BlockSpec(memory_space=pltpu.VMEM),
            pl.BlockSpec(memory_space=pl.ANY),
        ],
        out_specs=pl.BlockSpec(memory_space=pltpu.VMEM),
        scratch_shapes=[
            pltpu.VMEM((sources, packed, 2 * LANES), jnp.bfloat16),
            pltpu.VMEM((MODELS, chunks, packed, WIDE), jnp.bfloat16),
            pltpu.VMEM((LINES, length, MODELS, packed, 2 * LANES), jnp.bfloat16),
            pltpu.VMEM((chunks, LINES, length, MODELS, packed, WIDE), jnp.bfloat16),
            pltpu.VMEM((QUARTERS, rows // SUB, STACK * SUB, DEPTH), jnp.bfloat16),
            pltpu.VMEM((rows, cols), jnp.bfloat16),
            pltpu.VMEM((rows, cols), jnp.bfloat16),
            dma, dma((chunks,)), dma((chunks,)), dma((chunks,)), dma((chunks,)),
            dma, dma((chunks,)), dma((chunks,)), dma((chunks,)),
        ],
        compiler_params=pltpu.CompilerParams(
            collective_id=0, has_side_effects=True, vmem_limit_bytes=40 * 1024 * 1024),
        cost_estimate=pl.CostEstimate(
            flops=2 * STACK * rows * cols * DEPTH, bytes_accessed=12 * rows * cols, transcendentals=0),
        name="merge",
    )(slot_of, lengths, acts, grads, w_shard)


def solution(mesh):
    in_specs = (
        P(("groups", "mp"), "dp", None),
        P(("groups", "mp"), "dp", None),
        P(("groups", "mp"), "dp"),
        P(("groups", "mp"), None),
        P(("groups", "mp"), "dp", None),
    )
    out_specs = P(("groups", "dp"), "mp")

    def merge(activations, out_grads, slot_of, lengths, weights):
        tokens = activations.shape[1]
        rows = activations.shape[2] // mesh.shape["dp"]
        cols = out_grads.shape[2] // MODELS
        fits = (MODELS * QUARTERS * tokens == DEPTH and (QUARTERS * tokens // mesh.shape["dp"]) % 16 == 0
                and rows % SUB == 0 and rows == QUARTERS * LANES and cols % (QUARTERS * WIDE) == 0 and cols // (QUARTERS * WIDE) > 3)
        body = shards_kernel if fits else shards_general
        return jax.shard_map(body, mesh=mesh, in_specs=in_specs, out_specs=out_specs, check_vma=False)(
            activations, out_grads, slot_of, lengths, weights)

    return merge
```

```python
import functools

import jax
import jax.numpy as jnp
from jax import lax
from jax.experimental import pallas as pl
from jax.experimental.pallas import tpu as pltpu
from jax.sharding import PartitionSpec as P

EXAMPLES = 4
MODELS = 2
LANES = 128
DEPTH = 256
QUARTERS = 4
WIDE = 256
STACK = MODELS * EXAMPLES
SUB = 256
LINES = 2

fisher_eps = 1e-08


def place_rows(all_slots, left_all, right_all):
    count = all_slots.shape[0]
    row_of = jnp.zeros((count,), jnp.int32).at[all_slots].set(jnp.arange(count, dtype=jnp.int32))
    return (left_all[row_of], right_all[row_of])


def fisher_block(left_ord, right_ord, lens, span):
    count = left_ord.shape[0]
    ends = jnp.cumsum(lens)
    starts = ends - lens
    offsets = jnp.arange(span, dtype=jnp.int32)
    total = jnp.zeros((left_ord.shape[1], right_ord.shape[1]), jnp.float32)
    for example in range(EXAMPLES):
        begin = starts[example]
        clamped = jnp.minimum(begin, count - span)
        where_at = clamped + offsets
        keep = (where_at >= begin) & (where_at < begin + lens[example])
        left = lax.dynamic_slice_in_dim(left_ord, clamped, span, 0)
        left = jnp.where(keep[:, None], left, jnp.zeros((), jnp.bfloat16))
        right = lax.dynamic_slice_in_dim(right_ord, clamped, span, 0)
        grad = jnp.dot(left.T, right, preferred_element_type=jnp.float32)
        total = total + grad * grad
    return total


def shards_general(activations, out_grads, slot_of, lengths, weights):
    acts = activations[0]
    grads = out_grads[0]
    slots = slot_of[0]
    lens = lengths[0]
    w_shard = weights[0]
    span = lax.axis_size("dp") * acts.shape[0] // 3
    x_block = lax.all_to_all(acts, "dp", split_axis=1, concat_axis=0, tiled=True)
    all_grads, all_slots = (
        lax.all_gather(grads, "dp", axis=0, tiled=True),
        lax.all_gather(slots, "dp", axis=0, tiled=True),
    )
    left_ord, right_ord = place_rows(all_slots, x_block, all_grads)
    fisher = fisher_block(left_ord, right_ord, lens, span)
    weighted = fisher * w_shard.astype(jnp.float32)
    num_half, den_half = (
        lax.psum_scatter(weighted, "mp", scatter_dimension=1, tiled=True),
        lax.psum_scatter(fisher, "mp", scatter_dimension=1, tiled=True),
    )
    return num_half / (den_half + fisher_eps)


def chunk_rows(c, t, lhs, g_all, w_own, w_mate, store):
    at = pl.ds(pl.multiple_of(t * SUB, SUB), SUB)
    for q in range(QUARTERS):
        right = g_all[c].reshape(DEPTH, WIDE)
        fishers = []
        for h in range(MODELS):
            fisher = jnp.zeros((SUB, WIDE), jnp.float32)
            for e in range(EXAMPLES):
                v = h * EXAMPLES + e
                grad = jnp.dot(lhs[q, t, v * SUB:(v + 1) * SUB, :], right, preferred_element_type=jnp.float32)
                fisher = fisher + grad * grad
            fishers.append(fisher)
        own, other = fishers
        here = pl.ds(pl.multiple_of((c * QUARTERS + q) * WIDE, WIDE), WIDE)
        top = own * w_own[at, here].astype(jnp.float32) + other * w_mate[at, here].astype(jnp.float32)
        store(at, here, top / (own + other + fisher_eps))


def finish_kernel(early_ref, lhs, g_all, w_own, w_mate, out_ref, late, sem):
    rows, done = early_ref.shape
    step = QUARTERS * WIDE
    chunks, first = out_ref.shape[1] // step, done // step
    write = pltpu.make_async_copy(early_ref, out_ref.at[:, pl.ds(0, done)], sem.at[chunks - first])
    write.start()

    def out_copy(c):
        return pltpu.make_async_copy(
            late.at[:, pl.ds(pl.multiple_of((c - first) * step, LANES), step)],
            out_ref.at[:, pl.ds(pl.multiple_of(c * step, LANES), step)], sem.at[c - first])

    @pl.loop(first, chunks)
    def _(c):
        @pl.loop(0, rows // SUB)
        def _(t):
            def store(at, here, value):
                late[at, pl.ds(pl.multiple_of(here.start - done, WIDE), WIDE)] = value

            chunk_rows(c, t, lhs, g_all, w_own, w_mate, store)

        out_copy(c).start()

    @pl.loop(first, chunks)
    def _(c):
        out_copy(c).wait()

    write.wait()


def merge_kernel(sources, slots_ref, lens_ref, acts_ref, grads_ref, w_ref, early_ref, lhs, g_all, w_own, w_mate, x_ref, g_ref, x_all,
                 x_recv, line_recv, relay_recv, w_recv, own_sem, x_send, line_send, relay_send, w_send):
    mp, dp = lax.axis_index("mp"), lax.axis_index("dp")
    mate = 1 - mp
    line, spot = lax.rem(dp, LINES), lax.div(dp, LINES)
    length = sources // LINES
    rows, cols = w_own.shape
    chunks, early = g_ref.shape[1], early_ref.shape[1] // (QUARTERS * WIDE)
    step = QUARTERS * WIDE

    def send(src, dst, send_sem, recv_sem, to_mp, to_dp):
        return pltpu.make_async_remote_copy(
            src_ref=src, dst_ref=dst, send_sem=send_sem, recv_sem=recv_sem,
            device_id={"mp": to_mp, "dp": to_dp}, device_id_type=pl.DeviceIdType.MESH)

    def w_copy(c):
        return send(w_ref.at[:, pl.ds(pl.multiple_of(mate * cols + c * step, LANES), step)],
                    w_mate.at[:, pl.ds(pl.multiple_of(c * step, LANES), step)],
                    w_send.at[c], w_recv.at[c], mate, dp)

    def own_copy(c):
        return pltpu.make_async_copy(
            w_ref.at[:, pl.ds(pl.multiple_of(mp * cols + c * step, LANES), step)],
            w_own.at[:, pl.ds(pl.multiple_of(c * step, LANES), step)],
            own_sem.at[c])

    def line_copy(c, to_mp, to_dp):
        return send(g_ref.at[to_mp, c], g_all.at[c, line, spot, mp], line_send.at[c], line_recv.at[c], to_mp, to_dp)

    def relay_copy(c):
        return send(g_all.at[c, line], g_all.at[c, line], relay_send.at[c], relay_recv.at[c],
                    mp, spot * LINES + 1 - line)

    def relay(c):
        whole = g_all.at[c, line]
        pltpu.make_async_copy(whole, whole, line_recv.at[c]).wait()
        relay_copy(c).start()

    offsets = [(i, k) for k in range(sources) for i in range(MODELS) if (i, k) != (0, 0)]
    places = [(lax.rem(mp + i, MODELS), lax.rem(dp + k, sources)) for i, k in offsets]
    in_line = [(lax.rem(mp + i, MODELS), lax.rem(dp + k * LINES, sources))
               for k in range(length) for i in range(MODELS) if (i, k) != (0, 0)]

    barrier = pltpu.get_barrier_semaphore()
    for to_mp, to_dp in places:
        pl.semaphore_signal(barrier, inc=1, device_id={"mp": to_mp, "dp": to_dp},
                            device_id_type=pl.DeviceIdType.MESH)

    tokens = acts_ref.shape[0]
    packed = QUARTERS * tokens
    row = lax.broadcasted_iota(jnp.int32, (packed, LANES), 0)
    code = row // tokens
    for i in range(tokens):
        end, example = 0, 0
        for e in range(EXAMPLES - 1):
            end = end + lens_ref[0, e]
            example = example + jnp.where(slots_ref[0, i] >= end, 1, 0)
        code = code + jnp.where(row % tokens == i, (mp * EXAMPLES + example) * QUARTERS, 0)
    code = code.astype(jnp.float32).astype(jnp.bfloat16)

    def stacked(ref, start, width):
        parts = [ref[:, start + q * width:start + (q + 1) * width].astype(jnp.float32) for q in range(QUARTERS)]
        return jnp.concatenate(parts, axis=0).astype(jnp.bfloat16)

    for m in range(MODELS):
        for c in range(chunks):
            g_ref[m, c] = stacked(grads_ref, m * cols + c * step, WIDE)
    for k in range(sources):
        x_ref[k, :, :LANES] = stacked(acts_ref, k * rows, LANES)
        x_ref[k, :, LANES:] = code

    pltpu.make_async_copy(x_ref.at[dp], x_all.at[line, spot, mp], x_recv).start()

    @pl.loop(0, chunks)
    def _(c):
        pltpu.make_async_copy(g_ref.at[mp, c], g_all.at[c, line, spot, mp], line_recv.at[c]).start()
        own_copy(c).start()

    pl.semaphore_wait(barrier, len(places))
    for to_mp, to_dp in in_line:
        line_copy(0, to_mp, to_dp).start()
    for to_mp, to_dp in places:
        send(x_ref.at[to_dp], x_all.at[line, spot, mp], x_send, x_recv, to_mp, to_dp).start()
    w_copy(0).start()

    @pl.loop(1, chunks)
    def _(c):
        for to_mp, to_dp in in_line:
            line_copy(c, to_mp, to_dp).start()
        w_copy(c).start()

    relay(0)
    relay(1)

    pltpu.make_async_copy(x_all, x_all, x_recv).wait()
    arrived = x_all[...].reshape(DEPTH, 2 * LANES).astype(jnp.float32).T
    marks = arrived[LANES:LANES + 1, :]
    arrived = arrived[:LANES, :].astype(jnp.bfloat16)
    source = lax.broadcasted_iota(jnp.int32, (DEPTH, DEPTH), 0)
    target = lax.broadcasted_iota(jnp.int32, (DEPTH, DEPTH), 1)
    same = (source // packed == target // packed) & (source % tokens == target % tokens)
    for p in range(rows // LANES):
        spread = (same & (source % packed // tokens == p)).astype(jnp.float32).astype(jnp.bfloat16)
        left = jnp.dot(arrived, spread, preferred_element_type=jnp.float32).astype(jnp.bfloat16)
        t, base = p * LANES // SUB, p * LANES % SUB
        for q in range(QUARTERS):
            for v in range(STACK):
                which = lax.rem(mp + v // EXAMPLES, MODELS) * EXAMPLES + v % EXAMPLES
                keep = marks == (which * QUARTERS + q).astype(jnp.float32)
                lhs[q, t, v * SUB + base:v * SUB + base + LANES, :] = left * keep.astype(jnp.float32).astype(jnp.bfloat16)

    def arrive(c):
        other_line = g_all.at[c, 1 - line]
        pltpu.make_async_copy(other_line, other_line, relay_recv.at[c]).wait()
        own_copy(c).wait()
        w_copy(c).wait_recv()

    @pl.loop(0, early)
    def _(c):
        arrive(c)

        @pl.loop(0, rows // SUB)
        def _(t):
            @pl.when((t == rows // SUB - 1) & (c + 2 < chunks))
            def _():
                relay(c + 2)

            def store(at, here, value):
                early_ref[at, here] = value

            chunk_rows(c, t, lhs, g_all, w_own, w_mate, store)

    pl.loop(early, chunks)(arrive)

    blocks = lambda count: lhs.at[0, 0, pl.ds(0, count * packed)]
    pltpu.make_async_copy(blocks(len(places)), blocks(len(places)), x_send).wait()

    @pl.loop(0, chunks)
    def _(c):
        pltpu.make_async_copy(blocks(len(in_line)), blocks(len(in_line)), line_send.at[c]).wait()
        relay_copy(c).wait_send()
        w_copy(c).wait_send()


def shards_kernel(activations, out_grads, slot_of, lengths, weights):
    acts, grads, w_shard = activations[0], out_grads[0], weights[0]
    sources = lax.axis_size("dp")
    tokens, width = acts.shape
    rows = width // sources
    cols = grads.shape[1] // MODELS
    chunks = cols // (QUARTERS * WIDE)
    packed = QUARTERS * tokens
    length = sources // LINES
    dma = pltpu.SemaphoreType.DMA
    early = chunks - 2
    kept = [
        ((rows, early * QUARTERS * WIDE), jnp.float32),
        ((QUARTERS, rows // SUB, STACK * SUB, DEPTH), jnp.bfloat16),
        ((chunks, LINES, length, MODELS, packed, WIDE), jnp.bfloat16),
        ((rows, cols), jnp.bfloat16),
        ((rows, cols), jnp.bfloat16),
    ]
    vmem, anywhere = pl.BlockSpec(memory_space=pltpu.VMEM), pl.BlockSpec(memory_space=pl.ANY)
    smem = pl.BlockSpec(memory_space=pltpu.SMEM)
    handed = pl.pallas_call(
        functools.partial(merge_kernel, sources),
        out_shape=[pltpu.VMEM(*one) for one in kept],
        in_specs=[smem, smem, vmem, vmem, anywhere],
        out_specs=[vmem] * len(kept),
        scratch_shapes=[
            pltpu.VMEM((sources, packed, 2 * LANES), jnp.bfloat16),
            pltpu.VMEM((MODELS, chunks, packed, WIDE), jnp.bfloat16),
            pltpu.VMEM((LINES, length, MODELS, packed, 2 * LANES), jnp.bfloat16),
            dma, dma((chunks,)), dma((chunks,)), dma((chunks,)), dma((chunks,)),
            dma, dma((chunks,)), dma((chunks,)), dma((chunks,)),
        ],
        compiler_params=pltpu.CompilerParams(
            collective_id=0, has_side_effects=True, vmem_limit_bytes=12 * 1024 * 1024),
        name="merge",
    )(slot_of, lengths, acts, grads, w_shard)
    handed = [pltpu.with_memory_space_constraint(one, pltpu.VMEM) for one in handed]
    return pl.pallas_call(
        finish_kernel,
        out_shape=jax.ShapeDtypeStruct((rows, cols), jnp.float32),
        in_specs=[vmem] * len(kept),
        out_specs=anywhere,
        scratch_shapes=[
            pltpu.VMEM((rows, (chunks - early) * QUARTERS * WIDE), jnp.float32),
            dma((chunks - early + 1,)),
        ],
        compiler_params=pltpu.CompilerParams(vmem_limit_bytes=12 * 1024 * 1024),
        name="finish",
    )(*handed)


def solution(mesh):
    in_specs = (
        P(("groups", "mp"), "dp", None),
        P(("groups", "mp"), "dp", None),
        P(("groups", "mp"), "dp"),
        P(("groups", "mp"), None),
        P(("groups", "mp"), "dp", None),
    )
    out_specs = P(("groups", "dp"), "mp")

    def merge(activations, out_grads, slot_of, lengths, weights):
        tokens = activations.shape[1]
        rows = activations.shape[2] // mesh.shape["dp"]
        cols = out_grads.shape[2] // MODELS
        fits = (MODELS * QUARTERS * tokens == DEPTH and (QUARTERS * tokens // mesh.shape["dp"]) % 16 == 0
                and rows % SUB == 0 and rows == QUARTERS * LANES and cols % (QUARTERS * WIDE) == 0 and cols // (QUARTERS * WIDE) > 3)
        body = shards_kernel if fits else shards_general
        return jax.shard_map(body, mesh=mesh, in_specs=in_specs, out_specs=out_specs, check_vma=False)(
            activations, out_grads, slot_of, lengths, weights)

    return merge
```

```python
import functools

import jax
import jax.numpy as jnp
from jax import lax
from jax.experimental import pallas as pl
from jax.experimental.pallas import tpu as pltpu
from jax.sharding import PartitionSpec as P

EXAMPLES = 4
MODELS = 2
LANES = 128
DEPTH = 256
QUARTERS = 4
WIDE = 256
STACK = MODELS * EXAMPLES
SUB = 256
LINES = 2

fisher_eps = 1e-08


def place_rows(all_slots, left_all, right_all):
    count = all_slots.shape[0]
    row_of = jnp.zeros((count,), jnp.int32).at[all_slots].set(jnp.arange(count, dtype=jnp.int32))
    return (left_all[row_of], right_all[row_of])


def fisher_block(left_ord, right_ord, lens, span):
    count = left_ord.shape[0]
    ends = jnp.cumsum(lens)
    starts = ends - lens
    offsets = jnp.arange(span, dtype=jnp.int32)
    total = jnp.zeros((left_ord.shape[1], right_ord.shape[1]), jnp.float32)
    for example in range(EXAMPLES):
        begin = starts[example]
        clamped = jnp.minimum(begin, count - span)
        where_at = clamped + offsets
        keep = (where_at >= begin) & (where_at < begin + lens[example])
        left = lax.dynamic_slice_in_dim(left_ord, clamped, span, 0)
        left = jnp.where(keep[:, None], left, jnp.zeros((), jnp.bfloat16))
        right = lax.dynamic_slice_in_dim(right_ord, clamped, span, 0)
        grad = jnp.dot(left.T, right, preferred_element_type=jnp.float32)
        total = total + grad * grad
    return total


def shards_general(activations, out_grads, slot_of, lengths, weights):
    acts = activations[0]
    grads = out_grads[0]
    slots = slot_of[0]
    lens = lengths[0]
    w_shard = weights[0]
    span = lax.axis_size("dp") * acts.shape[0] // 3
    x_block = lax.all_to_all(acts, "dp", split_axis=1, concat_axis=0, tiled=True)
    all_grads, all_slots = (
        lax.all_gather(grads, "dp", axis=0, tiled=True),
        lax.all_gather(slots, "dp", axis=0, tiled=True),
    )
    left_ord, right_ord = place_rows(all_slots, x_block, all_grads)
    fisher = fisher_block(left_ord, right_ord, lens, span)
    weighted = fisher * w_shard.astype(jnp.float32)
    num_half, den_half = (
        lax.psum_scatter(weighted, "mp", scatter_dimension=1, tiled=True),
        lax.psum_scatter(fisher, "mp", scatter_dimension=1, tiled=True),
    )
    return num_half / (den_half + fisher_eps)


def chunk_rows(c, t, lhs, g_all, w_own, w_mate, store):
    at = pl.ds(pl.multiple_of(t * SUB, SUB), SUB)
    for q in range(QUARTERS):
        right = g_all[c].reshape(DEPTH, WIDE)
        fishers = []
        for h in range(MODELS):
            fisher = jnp.zeros((SUB, WIDE), jnp.float32)
            for e in range(EXAMPLES):
                v = h * EXAMPLES + e
                grad = jnp.dot(lhs[q, t, v * SUB:(v + 1) * SUB, :], right, preferred_element_type=jnp.float32)
                fisher = fisher + grad * grad
            fishers.append(fisher)
        own, other = fishers
        here = pl.ds(pl.multiple_of((c * QUARTERS + q) * WIDE, WIDE), WIDE)
        top = own * w_own[at, here].astype(jnp.float32) + other * w_mate[at, here].astype(jnp.float32)
        store(at, here, top / (own + other + fisher_eps))


def finish_kernel(early_ref, lhs, g_all, w_own, w_mate, out_ref, late, sem):
    rows, done = early_ref.shape
    step = QUARTERS * WIDE
    chunks, first = out_ref.shape[1] // step, done // step
    write = pltpu.make_async_copy(early_ref, out_ref.at[:, pl.ds(0, done)], sem.at[chunks - first])
    write.start()

    def out_copy(c):
        return pltpu.make_async_copy(
            late.at[:, pl.ds(pl.multiple_of((c - first) * step, LANES), step)],
            out_ref.at[:, pl.ds(pl.multiple_of(c * step, LANES), step)], sem.at[c - first])

    @pl.loop(first, chunks)
    def _(c):
        @pl.loop(0, rows // SUB)
        def _(t):
            def store(at, here, value):
                late[at, pl.ds(pl.multiple_of(here.start - done, WIDE), WIDE)] = value

            chunk_rows(c, t, lhs, g_all, w_own, w_mate, store)

        out_copy(c).start()

    @pl.loop(first, chunks)
    def _(c):
        out_copy(c).wait()

    write.wait()


def merge_kernel(sources, slots_ref, lens_ref, acts_ref, grads_ref, w_ref, early_ref, lhs, g_all, w_own, w_mate, x_ref, g_ref, x_all,
                 x_recv, line_recv, relay_recv, w_recv, own_sem, x_send, line_send, relay_send, w_send):
    mp, dp = lax.axis_index("mp"), lax.axis_index("dp")
    mate = 1 - mp
    line, spot = lax.rem(dp, LINES), lax.div(dp, LINES)
    length = sources // LINES
    rows, cols = w_own.shape
    chunks, early = g_ref.shape[1], early_ref.shape[1] // (QUARTERS * WIDE)
    step = QUARTERS * WIDE

    def send(src, dst, send_sem, recv_sem, to_mp, to_dp):
        return pltpu.make_async_remote_copy(
            src_ref=src, dst_ref=dst, send_sem=send_sem, recv_sem=recv_sem,
            device_id={"mp": to_mp, "dp": to_dp}, device_id_type=pl.DeviceIdType.MESH)

    def w_copy(c):
        return send(w_ref.at[:, pl.ds(pl.multiple_of(mate * cols + c * step, LANES), step)],
                    w_mate.at[:, pl.ds(pl.multiple_of(c * step, LANES), step)],
                    w_send.at[c], w_recv.at[c], mate, dp)

    def own_copy(c):
        return pltpu.make_async_copy(
            w_ref.at[:, pl.ds(pl.multiple_of(mp * cols + c * step, LANES), step)],
            w_own.at[:, pl.ds(pl.multiple_of(c * step, LANES), step)],
            own_sem.at[c])

    def line_copy(c, to_mp, to_dp):
        return send(g_ref.at[to_mp, c], g_all.at[c, line, spot, mp], line_send.at[c], line_recv.at[c], to_mp, to_dp)

    def relay_copy(c):
        return send(g_all.at[c, line], g_all.at[c, line], relay_send.at[c], relay_recv.at[c],
                    mp, spot * LINES + 1 - line)

    def relay(c):
        whole = g_all.at[c, line]
        pltpu.make_async_copy(whole, whole, line_recv.at[c]).wait()
        relay_copy(c).start()

    offsets = [(i, k) for k in range(sources) for i in range(MODELS) if (i, k) != (0, 0)]
    places = [(lax.rem(mp + i, MODELS), lax.rem(dp + k, sources)) for i, k in offsets]
    in_line = [(lax.rem(mp + i, MODELS), lax.rem(dp + k * LINES, sources))
               for k in range(length) for i in range(MODELS) if (i, k) != (0, 0)]

    barrier = pltpu.get_barrier_semaphore()
    for to_mp, to_dp in places:
        pl.semaphore_signal(barrier, inc=1, device_id={"mp": to_mp, "dp": to_dp},
                            device_id_type=pl.DeviceIdType.MESH)

    tokens = acts_ref.shape[0]
    packed = QUARTERS * tokens
    row = lax.broadcasted_iota(jnp.int32, (packed, LANES), 0)
    code = row // tokens
    for i in range(tokens):
        end, example = 0, 0
        for e in range(EXAMPLES - 1):
            end = end + lens_ref[0, e]
            example = example + jnp.where(slots_ref[0, i] >= end, 1, 0)
        code = code + jnp.where(row % tokens == i, (mp * EXAMPLES + example) * QUARTERS, 0)
    code = code.astype(jnp.float32).astype(jnp.bfloat16)

    def stacked(ref, start, width):
        parts = [ref[:, start + q * width:start + (q + 1) * width].astype(jnp.float32) for q in range(QUARTERS)]
        return jnp.concatenate(parts, axis=0).astype(jnp.bfloat16)

    for m in range(MODELS):
        for c in range(chunks):
            g_ref[m, c] = stacked(grads_ref, m * cols + c * step, WIDE)
    for k in range(sources):
        x_ref[k, :, :LANES] = stacked(acts_ref, k * rows, LANES)
        x_ref[k, :, LANES:] = code

    pltpu.make_async_copy(x_ref.at[dp], x_all.at[line, spot, mp], x_recv).start()

    @pl.loop(0, chunks)
    def _(c):
        pltpu.make_async_copy(g_ref.at[mp, c], g_all.at[c, line, spot, mp], line_recv.at[c]).start()
        own_copy(c).start()

    pl.semaphore_wait(barrier, len(places))
    for to_mp, to_dp in in_line:
        line_copy(0, to_mp, to_dp).start()
    for to_mp, to_dp in places:
        send(x_ref.at[to_dp], x_all.at[line, spot, mp], x_send, x_recv, to_mp, to_dp).start()
    w_copy(0).start()

    @pl.loop(1, chunks)
    def _(c):
        for to_mp, to_dp in in_line:
            line_copy(c, to_mp, to_dp).start()
        w_copy(c).start()

    relay(0)
    relay(1)

    pltpu.make_async_copy(x_all, x_all, x_recv).wait()
    arrived = x_all[...].reshape(DEPTH, 2 * LANES).astype(jnp.float32).T
    marks = arrived[LANES:LANES + 1, :]
    arrived = arrived[:LANES, :].astype(jnp.bfloat16)
    source = lax.broadcasted_iota(jnp.int32, (DEPTH, DEPTH), 0)
    target = lax.broadcasted_iota(jnp.int32, (DEPTH, DEPTH), 1)
    same = (source // packed == target // packed) & (source % tokens == target % tokens)
    for p in range(rows // LANES):
        spread = (same & (source % packed // tokens == p)).astype(jnp.float32).astype(jnp.bfloat16)
        left = jnp.dot(arrived, spread, preferred_element_type=jnp.float32).astype(jnp.bfloat16)
        t, base = p * LANES // SUB, p * LANES % SUB
        for q in range(QUARTERS):
            for v in range(STACK):
                which = lax.rem(mp + v // EXAMPLES, MODELS) * EXAMPLES + v % EXAMPLES
                keep = marks == (which * QUARTERS + q).astype(jnp.float32)
                lhs[q, t, v * SUB + base:v * SUB + base + LANES, :] = left * keep.astype(jnp.float32).astype(jnp.bfloat16)

    def arrive(c):
        other_line = g_all.at[c, 1 - line]
        pltpu.make_async_copy(other_line, other_line, relay_recv.at[c]).wait()
        own_copy(c).wait()
        w_copy(c).wait_recv()

    @pl.loop(0, early)
    def _(c):
        arrive(c)

        @pl.loop(0, rows // SUB)
        def _(t):
            part = c * (rows // SUB) + t

            @pl.when(part == 1)
            def _():
                relay(2)

            @pl.when((part >= 3) & (part < chunks))
            def _():
                relay(part)

            def store(at, here, value):
                early_ref[at, here] = value

            chunk_rows(c, t, lhs, g_all, w_own, w_mate, store)

    pl.loop(early, chunks)(arrive)

    blocks = lambda count: lhs.at[0, 0, pl.ds(0, count * packed)]
    pltpu.make_async_copy(blocks(len(places)), blocks(len(places)), x_send).wait()

    @pl.loop(0, chunks)
    def _(c):
        pltpu.make_async_copy(blocks(len(in_line)), blocks(len(in_line)), line_send.at[c]).wait()
        relay_copy(c).wait_send()
        w_copy(c).wait_send()


def shards_kernel(activations, out_grads, slot_of, lengths, weights):
    acts, grads, w_shard = activations[0], out_grads[0], weights[0]
    sources = lax.axis_size("dp")
    tokens, width = acts.shape
    rows = width // sources
    cols = grads.shape[1] // MODELS
    chunks = cols // (QUARTERS * WIDE)
    packed = QUARTERS * tokens
    length = sources // LINES
    dma = pltpu.SemaphoreType.DMA
    early = chunks - 2
    kept = [
        ((rows, early * QUARTERS * WIDE), jnp.float32),
        ((QUARTERS, rows // SUB, STACK * SUB, DEPTH), jnp.bfloat16),
        ((chunks, LINES, length, MODELS, packed, WIDE), jnp.bfloat16),
        ((rows, cols), jnp.bfloat16),
        ((rows, cols), jnp.bfloat16),
    ]
    vmem, anywhere = pl.BlockSpec(memory_space=pltpu.VMEM), pl.BlockSpec(memory_space=pl.ANY)
    smem = pl.BlockSpec(memory_space=pltpu.SMEM)
    handed = pl.pallas_call(
        functools.partial(merge_kernel, sources),
        out_shape=[pltpu.VMEM(*one) for one in kept],
        in_specs=[smem, smem, vmem, vmem, anywhere],
        out_specs=[vmem] * len(kept),
        scratch_shapes=[
            pltpu.VMEM((sources, packed, 2 * LANES), jnp.bfloat16),
            pltpu.VMEM((MODELS, chunks, packed, WIDE), jnp.bfloat16),
            pltpu.VMEM((LINES, length, MODELS, packed, 2 * LANES), jnp.bfloat16),
            dma, dma((chunks,)), dma((chunks,)), dma((chunks,)), dma((chunks,)),
            dma, dma((chunks,)), dma((chunks,)), dma((chunks,)),
        ],
        compiler_params=pltpu.CompilerParams(
            collective_id=0, has_side_effects=True, vmem_limit_bytes=12 * 1024 * 1024),
        name="merge",
    )(*[pltpu.with_memory_space_constraint(one, pltpu.HBM) for one in (slot_of, lengths, acts, grads)], w_shard)
    handed = [pltpu.with_memory_space_constraint(one, pltpu.VMEM) for one in handed]
    return pl.pallas_call(
        finish_kernel,
        out_shape=jax.ShapeDtypeStruct((rows, cols), jnp.float32),
        in_specs=[vmem] * len(kept),
        out_specs=anywhere,
        scratch_shapes=[
            pltpu.VMEM((rows, (chunks - early) * QUARTERS * WIDE), jnp.float32),
            dma((chunks - early + 1,)),
        ],
        compiler_params=pltpu.CompilerParams(vmem_limit_bytes=12 * 1024 * 1024),
        name="finish",
    )(*handed)


def solution(mesh):
    in_specs = (
        P(("groups", "mp"), "dp", None),
        P(("groups", "mp"), "dp", None),
        P(("groups", "mp"), "dp"),
        P(("groups", "mp"), None),
        P(("groups", "mp"), "dp", None),
    )
    out_specs = P(("groups", "dp"), "mp")

    def merge(activations, out_grads, slot_of, lengths, weights):
        tokens = activations.shape[1]
        rows = activations.shape[2] // mesh.shape["dp"]
        cols = out_grads.shape[2] // MODELS
        fits = (MODELS * QUARTERS * tokens == DEPTH and (QUARTERS * tokens // mesh.shape["dp"]) % 16 == 0
                and rows % SUB == 0 and rows == QUARTERS * LANES and cols % (QUARTERS * WIDE) == 0 and cols // (QUARTERS * WIDE) > 3)
        body = shards_kernel if fits else shards_general
        return jax.shard_map(body, mesh=mesh, in_specs=in_specs, out_specs=out_specs, check_vma=False)(
            activations, out_grads, slot_of, lengths, weights)

    return merge
```

```python
import functools

import jax
import jax.numpy as jnp
from jax import lax
from jax.experimental import pallas as pl
from jax.experimental.pallas import tpu as pltpu
from jax.sharding import PartitionSpec as P

EXAMPLES = 4
MODELS = 2
LANES = 128
DEPTH = 256
QUARTERS = 4
WIDE = 256
STACK = MODELS * EXAMPLES
SUB = 256
LINES = 2

fisher_eps = 1e-08


def place_rows(all_slots, left_all, right_all):
    count = all_slots.shape[0]
    row_of = jnp.zeros((count,), jnp.int32).at[all_slots].set(jnp.arange(count, dtype=jnp.int32))
    return (left_all[row_of], right_all[row_of])


def fisher_block(left_ord, right_ord, lens, span):
    count = left_ord.shape[0]
    ends = jnp.cumsum(lens)
    starts = ends - lens
    offsets = jnp.arange(span, dtype=jnp.int32)
    total = jnp.zeros((left_ord.shape[1], right_ord.shape[1]), jnp.float32)
    for example in range(EXAMPLES):
        begin = starts[example]
        clamped = jnp.minimum(begin, count - span)
        where_at = clamped + offsets
        keep = (where_at >= begin) & (where_at < begin + lens[example])
        left = lax.dynamic_slice_in_dim(left_ord, clamped, span, 0)
        left = jnp.where(keep[:, None], left, jnp.zeros((), jnp.bfloat16))
        right = lax.dynamic_slice_in_dim(right_ord, clamped, span, 0)
        grad = jnp.dot(left.T, right, preferred_element_type=jnp.float32)
        total = total + grad * grad
    return total


def shards_general(activations, out_grads, slot_of, lengths, weights):
    acts = activations[0]
    grads = out_grads[0]
    slots = slot_of[0]
    lens = lengths[0]
    w_shard = weights[0]
    span = lax.axis_size("dp") * acts.shape[0] // 3
    x_block = lax.all_to_all(acts, "dp", split_axis=1, concat_axis=0, tiled=True)
    all_grads, all_slots = (
        lax.all_gather(grads, "dp", axis=0, tiled=True),
        lax.all_gather(slots, "dp", axis=0, tiled=True),
    )
    left_ord, right_ord = place_rows(all_slots, x_block, all_grads)
    fisher = fisher_block(left_ord, right_ord, lens, span)
    weighted = fisher * w_shard.astype(jnp.float32)
    num_half, den_half = (
        lax.psum_scatter(weighted, "mp", scatter_dimension=1, tiled=True),
        lax.psum_scatter(fisher, "mp", scatter_dimension=1, tiled=True),
    )
    return num_half / (den_half + fisher_eps)


def chunk_rows(c, t, lhs, g_all, w_own, w_mate, store):
    at = pl.ds(pl.multiple_of(t * SUB, SUB), SUB)
    for q in range(QUARTERS):
        right = g_all[c].reshape(DEPTH, WIDE)
        fishers = []
        for h in range(MODELS):
            fisher = jnp.zeros((SUB, WIDE), jnp.float32)
            for e in range(EXAMPLES):
                v = h * EXAMPLES + e
                grad = jnp.dot(lhs[q, t, v * SUB:(v + 1) * SUB, :], right, preferred_element_type=jnp.float32)
                fisher = fisher + grad * grad
            fishers.append(fisher)
        own, other = fishers
        here = pl.ds(pl.multiple_of((c * QUARTERS + q) * WIDE, WIDE), WIDE)
        top = own * w_own[at, here].astype(jnp.float32) + other * w_mate[at, here].astype(jnp.float32)
        store(at, here, top / (own + other + fisher_eps))


def finish_kernel(early_ref, lhs, g_all, w_own, w_mate, out_ref, late, sem):
    rows, done = early_ref.shape
    step = QUARTERS * WIDE
    chunks, first = out_ref.shape[1] // step, done // step
    write = pltpu.make_async_copy(early_ref, out_ref.at[:, pl.ds(0, done)], sem.at[chunks - first])
    write.start()

    def out_copy(c):
        return pltpu.make_async_copy(
            late.at[:, pl.ds(pl.multiple_of((c - first) * step, LANES), step)],
            out_ref.at[:, pl.ds(pl.multiple_of(c * step, LANES), step)], sem.at[c - first])

    @pl.loop(first, chunks)
    def _(c):
        @pl.loop(0, rows // SUB)
        def _(t):
            def store(at, here, value):
                late[at, pl.ds(pl.multiple_of(here.start - done, WIDE), WIDE)] = value

            chunk_rows(c, t, lhs, g_all, w_own, w_mate, store)

        out_copy(c).start()

    @pl.loop(first, chunks)
    def _(c):
        out_copy(c).wait()

    write.wait()


def merge_kernel(sources, slots_ref, lens_ref, acts_ref, grads_ref, w_ref, early_ref, lhs, g_all, w_own, w_mate, x_ref, g_ref, x_all,
                 x_recv, line_recv, relay_recv, w_recv, own_sem, x_send, line_send, relay_send, w_send):
    mp, dp = lax.axis_index("mp"), lax.axis_index("dp")
    mate = 1 - mp
    line, spot = lax.rem(dp, LINES), lax.div(dp, LINES)
    length = sources // LINES
    rows, cols = w_own.shape
    chunks, early = g_ref.shape[1], early_ref.shape[1] // (QUARTERS * WIDE)
    step = QUARTERS * WIDE

    def send(src, dst, send_sem, recv_sem, to_mp, to_dp):
        return pltpu.make_async_remote_copy(
            src_ref=src, dst_ref=dst, send_sem=send_sem, recv_sem=recv_sem,
            device_id={"mp": to_mp, "dp": to_dp}, device_id_type=pl.DeviceIdType.MESH)

    def w_copy(c):
        return send(w_ref.at[:, pl.ds(pl.multiple_of(mate * cols + c * step, LANES), step)],
                    w_mate.at[:, pl.ds(pl.multiple_of(c * step, LANES), step)],
                    w_send.at[c], w_recv.at[c], mate, dp)

    def own_copy(c):
        return pltpu.make_async_copy(
            w_ref.at[:, pl.ds(pl.multiple_of(mp * cols + c * step, LANES), step)],
            w_own.at[:, pl.ds(pl.multiple_of(c * step, LANES), step)],
            own_sem.at[c])

    def line_copy(c, to_mp, to_dp):
        return send(g_ref.at[to_mp, c], g_all.at[c, line, spot, mp], line_send.at[c], line_recv.at[c], to_mp, to_dp)

    def relay_copy(c):
        return send(g_all.at[c, line], g_all.at[c, line], relay_send.at[c], relay_recv.at[c],
                    mp, spot * LINES + 1 - line)

    def relay(c):
        whole = g_all.at[c, line]
        pltpu.make_async_copy(whole, whole, line_recv.at[c]).wait()
        relay_copy(c).start()

    offsets = [(i, k) for k in range(sources) for i in range(MODELS) if (i, k) != (0, 0)]
    places = [(lax.rem(mp + i, MODELS), lax.rem(dp + k, sources)) for i, k in offsets]
    in_line = [(lax.rem(mp + i, MODELS), lax.rem(dp + k * LINES, sources))
               for k in range(length) for i in range(MODELS) if (i, k) != (0, 0)]

    barrier = pltpu.get_barrier_semaphore()
    for to_mp, to_dp in places:
        pl.semaphore_signal(barrier, inc=1, device_id={"mp": to_mp, "dp": to_dp},
                            device_id_type=pl.DeviceIdType.MESH)

    tokens = acts_ref.shape[0]
    packed = QUARTERS * tokens
    row = lax.broadcasted_iota(jnp.int32, (packed, LANES), 0)
    code = row // tokens
    for i in range(tokens):
        end, example = 0, 0
        for e in range(EXAMPLES - 1):
            end = end + lens_ref[0, e]
            example = example + jnp.where(slots_ref[0, i] >= end, 1, 0)
        code = code + jnp.where(row % tokens == i, (mp * EXAMPLES + example) * QUARTERS, 0)
    code = code.astype(jnp.float32).astype(jnp.bfloat16)

    def stacked(ref, start, width):
        parts = [ref[:, start + q * width:start + (q + 1) * width].astype(jnp.float32) for q in range(QUARTERS)]
        return jnp.concatenate(parts, axis=0).astype(jnp.bfloat16)

    for m in range(MODELS):
        for c in range(chunks):
            g_ref[m, c] = stacked(grads_ref, m * cols + c * step, WIDE)
    for k in range(sources):
        x_ref[k, :, :LANES] = stacked(acts_ref, k * rows, LANES)
        x_ref[k, :, LANES:] = code

    pltpu.make_async_copy(x_ref.at[dp], x_all.at[line, spot, mp], x_recv).start()

    @pl.loop(0, chunks)
    def _(c):
        pltpu.make_async_copy(g_ref.at[mp, c], g_all.at[c, line, spot, mp], line_recv.at[c]).start()
        own_copy(c).start()

    pl.semaphore_wait(barrier, len(places))
    for to_mp, to_dp in in_line:
        line_copy(0, to_mp, to_dp).start()
    for to_mp, to_dp in places:
        send(x_ref.at[to_dp], x_all.at[line, spot, mp], x_send, x_recv, to_mp, to_dp).start()
    w_copy(0).start()

    @pl.loop(1, chunks)
    def _(c):
        for to_mp, to_dp in in_line:
            line_copy(c, to_mp, to_dp).start()
        w_copy(c).start()

    relay(0)

    pltpu.make_async_copy(x_all, x_all, x_recv).wait()
    arrived = x_all[...].reshape(DEPTH, 2 * LANES).astype(jnp.float32).T
    marks = arrived[LANES:LANES + 1, :]
    arrived = arrived[:LANES, :].astype(jnp.bfloat16)
    source = lax.broadcasted_iota(jnp.int32, (DEPTH, DEPTH), 0)
    target = lax.broadcasted_iota(jnp.int32, (DEPTH, DEPTH), 1)
    same = (source // packed == target // packed) & (source % tokens == target % tokens)
    for p in range(rows // LANES):
        spread = (same & (source % packed // tokens == p)).astype(jnp.float32).astype(jnp.bfloat16)
        left = jnp.dot(arrived, spread, preferred_element_type=jnp.float32).astype(jnp.bfloat16)
        t, base = p * LANES // SUB, p * LANES % SUB
        for q in range(QUARTERS):
            for v in range(STACK):
                which = lax.rem(mp + v // EXAMPLES, MODELS) * EXAMPLES + v % EXAMPLES
                keep = marks == (which * QUARTERS + q).astype(jnp.float32)
                lhs[q, t, v * SUB + base:v * SUB + base + LANES, :] = left * keep.astype(jnp.float32).astype(jnp.bfloat16)

    relay(1)

    def arrive(c):
        other_line = g_all.at[c, 1 - line]
        pltpu.make_async_copy(other_line, other_line, relay_recv.at[c]).wait()
        own_copy(c).wait()
        w_copy(c).wait_recv()

    @pl.loop(0, early)
    def _(c):
        arrive(c)

        @pl.loop(0, rows // SUB)
        def _(t):
            part = c * (rows // SUB) + t

            @pl.when(part == 1)
            def _():
                relay(2)

            @pl.when((part >= 3) & (part < chunks))
            def _():
                relay(part)

            def store(at, here, value):
                early_ref[at, here] = value

            chunk_rows(c, t, lhs, g_all, w_own, w_mate, store)

    pl.loop(early, chunks)(arrive)

    blocks = lambda count: lhs.at[0, 0, pl.ds(0, count * packed)]
    pltpu.make_async_copy(blocks(len(places)), blocks(len(places)), x_send).wait()

    @pl.loop(0, chunks)
    def _(c):
        pltpu.make_async_copy(blocks(len(in_line)), blocks(len(in_line)), line_send.at[c]).wait()
        relay_copy(c).wait_send()
        w_copy(c).wait_send()


def shards_kernel(activations, out_grads, slot_of, lengths, weights):
    acts, grads, w_shard = activations[0], out_grads[0], weights[0]
    sources = lax.axis_size("dp")
    tokens, width = acts.shape
    rows = width // sources
    cols = grads.shape[1] // MODELS
    chunks = cols // (QUARTERS * WIDE)
    packed = QUARTERS * tokens
    length = sources // LINES
    dma = pltpu.SemaphoreType.DMA
    early = chunks - 2
    kept = [
        ((rows, early * QUARTERS * WIDE), jnp.float32),
        ((QUARTERS, rows // SUB, STACK * SUB, DEPTH), jnp.bfloat16),
        ((chunks, LINES, length, MODELS, packed, WIDE), jnp.bfloat16),
        ((rows, cols), jnp.bfloat16),
        ((rows, cols), jnp.bfloat16),
    ]
    vmem, anywhere = pl.BlockSpec(memory_space=pltpu.VMEM), pl.BlockSpec(memory_space=pl.ANY)
    smem = pl.BlockSpec(memory_space=pltpu.SMEM)
    handed = pl.pallas_call(
        functools.partial(merge_kernel, sources),
        out_shape=[pltpu.VMEM(*one) for one in kept],
        in_specs=[smem, smem, vmem, vmem, anywhere],
        out_specs=[vmem] * len(kept),
        scratch_shapes=[
            pltpu.VMEM((sources, packed, 2 * LANES), jnp.bfloat16),
            pltpu.VMEM((MODELS, chunks, packed, WIDE), jnp.bfloat16),
            pltpu.VMEM((LINES, length, MODELS, packed, 2 * LANES), jnp.bfloat16),
            dma, dma((chunks,)), dma((chunks,)), dma((chunks,)), dma((chunks,)),
            dma, dma((chunks,)), dma((chunks,)), dma((chunks,)),
        ],
        compiler_params=pltpu.CompilerParams(
            collective_id=0, has_side_effects=True, vmem_limit_bytes=12 * 1024 * 1024),
        name="merge",
    )(*[pltpu.with_memory_space_constraint(one, pltpu.HBM) for one in (slot_of, lengths, acts, grads)], w_shard)
    handed = [pltpu.with_memory_space_constraint(one, pltpu.VMEM) for one in handed]
    return pl.pallas_call(
        finish_kernel,
        out_shape=jax.ShapeDtypeStruct((rows, cols), jnp.float32),
        in_specs=[vmem] * len(kept),
        out_specs=anywhere,
        scratch_shapes=[
            pltpu.VMEM((rows, (chunks - early) * QUARTERS * WIDE), jnp.float32),
            dma((chunks - early + 1,)),
        ],
        compiler_params=pltpu.CompilerParams(vmem_limit_bytes=12 * 1024 * 1024),
        name="finish",
    )(*handed)


def solution(mesh):
    in_specs = (
        P(("groups", "mp"), "dp", None),
        P(("groups", "mp"), "dp", None),
        P(("groups", "mp"), "dp"),
        P(("groups", "mp"), None),
        P(("groups", "mp"), "dp", None),
    )
    out_specs = P(("groups", "dp"), "mp")

    def merge(activations, out_grads, slot_of, lengths, weights):
        tokens = activations.shape[1]
        rows = activations.shape[2] // mesh.shape["dp"]
        cols = out_grads.shape[2] // MODELS
        fits = (MODELS * QUARTERS * tokens == DEPTH and (QUARTERS * tokens // mesh.shape["dp"]) % 16 == 0
                and rows % SUB == 0 and rows == QUARTERS * LANES and cols % (QUARTERS * WIDE) == 0 and cols // (QUARTERS * WIDE) > 3)
        body = shards_kernel if fits else shards_general
        return jax.shard_map(body, mesh=mesh, in_specs=in_specs, out_specs=out_specs, check_vma=False)(
            activations, out_grads, slot_of, lengths, weights)

    return merge
```
